32 devices in a mesh: parts: 2 (over y), seq: 8 (over z, x), head: 2 (over core).
Axes of the slice: x: 2, y: 2, z: 4, core: 2. Of those that a mesh axis runs over, the one named last changes fastest.
Arguments:
- frames: bfloat16 [4096, 1024], P(('parts', 'seq'), 'head'), parts along dimension 0, may hold values from -40 to 40
- w_query: bfloat16 [1024, 1024], P(None, 'head'), may hold values from -0.1875 to 0.1875
- w_key: bfloat16 [1024, 1024], P(None, 'head'), may hold values from -0.1875 to 0.1875
- w_value: bfloat16 [1024, 1024], P(None, 'head'), may hold values from -0.1875 to 0.1875
- down_bank: bfloat16 [8, 1024, 128], P(None, 'seq'), may hold values from -0.1875 to 0.1875
- up_bank: bfloat16 [8, 128, 1024], P(None, 'seq', 'head'), may hold values from -0.75 to 0.75
- bank_row: int32 [8], replicated, may hold values from 0 to 7, each once
- lang_ids: int32 [16], P('parts'), parts along dimension 0, may hold values from 0 to 7, as said below
- seg_ids: int32 [16], P('parts'), parts along dimension 0, may hold values from 0 to 1, as said below
- lookback: int32 [16], P('parts'), parts along dimension 0, may hold values from 0 to 3, as said below
Outputs:
- context: bfloat16 [4096, 1024], P(('parts', 'seq'), 'head'), parts along dimension 0
The draws below stay inside these ranges and needn't reach their ends.
There are 2 independent parts, one for each index of `parts`. The reference program is written for one: setup_inputs(seed, part) draws one part's arguments, and reference() takes and returns one part's arrays. A program takes and returns all parts, laid end to end along the dimension named above; an argument that names none is the same for every part. Nothing has to cross between parts.
Inputs may be any that keep to these rules, and one draw needn't show every extreme that they name: `seg_ids`: blocks of one utterance are consecutive: the number is 0 at the first block and never falls; the largest number is reached at the last block. `lang_ids`: all blocks of one utterance have the same language; the last utterance has language 8 - 1. `bank_row`: each language names a different bank row. `lookback`: the value 3 is reached in every draw.
All inputs are finite; a program needn't handle non-finite values.
Results may differ from the reference program's by a relative error of at most 0.0093.
Values may be sent and summed in bfloat16 or wider, within the bound.
A program may use at most 64 MiB of HBM per device.

```python
import math
import jax
import jax.numpy as jnp
from jax import lax

D = 1024
H = 16
HD = 64
R = 64
BLK = 256
FR_DEV = 256
FRAMES = 2048
BPD = 1
NBLK = 8
LOOK = 3
LANG = 8
N_SEQ = 8


def draw_frames(key, part):
    gaussian = jnp.clip(jax.random.normal(jax.random.fold_in(key, 1), (FRAMES, D), jnp.float32), -4.0, 4.0)
    return gaussian.astype(jnp.bfloat16)


def weight_pair(key):
    shared_normal = jnp.clip(jax.random.normal(jax.random.fold_in(key, 21), (D, D), jnp.float32), -6.0, 6.0)
    own_normal = jnp.clip(jax.random.normal(jax.random.fold_in(key, 22), (D, D), jnp.float32), -6.0, 6.0)
    return (shared_normal, own_normal)


def draw_w_query(key, part):
    shared_normal, own_normal = weight_pair(key)
    return (shared_normal / math.sqrt(D)).astype(jnp.bfloat16)


def draw_w_key(key, part):
    shared_normal, own_normal = weight_pair(key)
    return (own_normal / math.sqrt(D)).astype(jnp.bfloat16)


def block_tables(key):
    utterances = NBLK // (4 * BPD)
    shuffled = jax.random.permutation(jax.random.fold_in(key, 31), NBLK - 1) + 1
    cuts = shuffled[:utterances - 1]
    openings = jnp.zeros((NBLK,), jnp.int32).at[0].set(1).at[cuts].set(1)
    segments = jnp.cumsum(openings) - 1
    popular = jax.random.randint(jax.random.fold_in(key, 32), (4,), 0, LANG)
    which_popular = jax.random.randint(jax.random.fold_in(key, 33), (NBLK,), 0, 4)
    any_language = jax.random.randint(jax.random.fold_in(key, 34), (NBLK,), 0, LANG)
    favour = jax.random.randint(jax.random.fold_in(key, 35), (NBLK,), 0, 2) == 0
    seg_language = jnp.where(favour, popular[which_popular], any_language)
    last_segment = segments[NBLK - 1]
    seg_language = jnp.where(jnp.arange(NBLK, dtype=jnp.int32) == last_segment, LANG - 1, seg_language)
    return (segments.astype(jnp.int32), seg_language[segments].astype(jnp.int32))


def draw_seg_ids(key, part):
    segments, languages = block_tables(key)
    return segments


def draw_lang_ids(key, part):
    segments, languages = block_tables(key)
    return languages


def draw_lookback(key, part):
    longest = jax.random.randint(jax.random.fold_in(key, 41), (NBLK,), 0, 4) == 0
    spread = jax.random.randint(jax.random.fold_in(key, 42), (NBLK,), 0, LOOK + 1)
    reach_draw = jnp.where(longest, LOOK, spread)
    return reach_draw.at[NBLK - 1].set(LOOK).astype(jnp.int32)


def shard_levels(own_key, extent, pieces, low, top_value):
    def one(dim, parts):
        heights = jax.random.uniform(jax.random.fold_in(jax.random.fold_in(own_key, 6), dim), (parts,), jnp.float32, low / len(pieces), top_value / len(pieces))
        return jnp.repeat(jnp.exp(heights), extent[dim] // parts).reshape((-1,) + (1,) * (len(extent) - dim - 1))

    loudness = one(*pieces[0])
    for cut in pieces[1:]:
        loudness = loudness * one(*cut)
    return loudness


def bell_draw(stream_key, extent, deviation, limit, cuts=(), kind=jnp.bfloat16):
    result = jax.random.normal(stream_key, extent, jnp.float32) * deviation
    if len(cuts) > 0:
        result = shard_levels(stream_key, extent, cuts, -0.22, 0.18) * result
    return jnp.clip(result, min=-limit, max=limit).astype(kind)


def setup_inputs(seed: int = 0, part: int = 0) -> dict:
    keys = jax.random.split(jax.random.key(seed), 11)
    part_splits = jax.random.split(jax.random.fold_in(keys[10], part), 11)
    return {
        "frames": draw_frames(jax.random.fold_in(jax.random.fold_in(keys[10], part), 71), part),
        "w_query": draw_w_query(jax.random.fold_in(keys[10], 71), part),
        "w_key": draw_w_key(jax.random.fold_in(keys[10], 71), part),
        "w_value": bell_draw(keys[3], (D, D), D ** -0.5, 0.1875, ((1, 2),)),
        "down_bank": bell_draw(keys[4], (LANG, D, 2 * R), D ** -0.5, 0.1875, ((1, 8),)),
        "up_bank": bell_draw(keys[5], (LANG, 2 * R, D), R ** -0.5, 0.75, ((1, 8), (2, 2))),
        "bank_row": jax.random.permutation(keys[6], LANG).astype(jnp.int32),
        "lang_ids": draw_lang_ids(jax.random.fold_in(jax.random.fold_in(keys[10], part), 71), part),
        "seg_ids": draw_seg_ids(jax.random.fold_in(jax.random.fold_in(keys[10], part), 71), part),
        "lookback": draw_lookback(jax.random.fold_in(jax.random.fold_in(keys[10], part), 71), part),
    }


NEG_LARGE = -1.0e30


def reference(frames, w_query, w_key, w_value, down_bank, up_bank, bank_row, lang_ids, seg_ids, lookback):
    queries = jnp.dot(frames, w_query, preferred_element_type=jnp.float32).astype(jnp.bfloat16)
    queries = lax.optimization_barrier(queries)
    rows_used = jnp.take(bank_row, lang_ids, axis=0).astype(jnp.int32)
    block_rows = frames.reshape(NBLK, BLK, D).astype(jnp.float32)
    down_used = jnp.take(down_bank, rows_used, axis=0).astype(jnp.float32)
    lowrank = jnp.einsum("bfd,bdr->bfr", block_rows, down_used).astype(jnp.bfloat16)
    lowrank = lax.optimization_barrier(lowrank).astype(jnp.float32)
    up_used = jnp.take(up_bank, rows_used, axis=0).astype(jnp.float32)
    key_extra = jnp.einsum("bfr,brc->bfc", lowrank[:, :, :R], up_used[:, :R]).reshape(FRAMES, D)
    value_extra = jnp.einsum("bfr,brc->bfc", lowrank[:, :, R:], up_used[:, R:]).reshape(FRAMES, D)
    own_keys = (jnp.dot(frames, w_key, preferred_element_type=jnp.float32) + key_extra).astype(jnp.bfloat16)
    own_values = (jnp.dot(frames, w_value, preferred_element_type=jnp.float32) + value_extra).astype(jnp.bfloat16)
    own_keys = lax.optimization_barrier(own_keys)
    own_values = lax.optimization_barrier(own_values)
    pad_keys = jnp.concatenate([jnp.zeros((3 * FR_DEV, D), own_keys.dtype), own_keys], axis=0)
    pad_values = jnp.concatenate([jnp.zeros((3 * FR_DEV, D), own_values.dtype), own_values], axis=0)
    pad_seg = jnp.concatenate([jnp.full((3 * BPD,), -1, jnp.int32), seg_ids.astype(jnp.int32)])

    def one_shard(shard_index):
        query_first = (shard_index * BPD).astype(jnp.int32)
        query_blocks = query_first + jnp.arange(BPD, dtype=jnp.int32)
        key_blocks = query_first - 3 * BPD + jnp.arange(4 * BPD, dtype=jnp.int32)
        query_seg = lax.dynamic_slice_in_dim(seg_ids.astype(jnp.int32), query_first, BPD)
        query_reach = lax.dynamic_slice_in_dim(lookback.astype(jnp.int32), query_first, BPD)
        key_seg = lax.dynamic_slice_in_dim(pad_seg, query_first, 4 * BPD)
        allowed = key_blocks[None, :] >= query_blocks[:, None] - query_reach[:, None]
        allowed = allowed & (key_blocks[None, :] <= query_blocks[:, None])
        allowed = allowed & (key_seg[None, :] == query_seg[:, None]) & (key_blocks[None, :] >= 0)
        frame_mask = jnp.broadcast_to(allowed[:, None, :, None], (BPD, BLK, 4 * BPD, BLK)).reshape(FR_DEV, 4 * FR_DEV)
        frame_first = (shard_index * FR_DEV).astype(jnp.int32)
        query_part = lax.dynamic_slice_in_dim(queries, frame_first, FR_DEV).reshape(FR_DEV, H, HD).astype(jnp.float32)
        key_part = lax.dynamic_slice_in_dim(pad_keys, frame_first, 4 * FR_DEV).reshape(4 * FR_DEV, H, HD).astype(jnp.float32)
        value_part = lax.dynamic_slice_in_dim(pad_values, frame_first, 4 * FR_DEV).reshape(4 * FR_DEV, H, HD).astype(jnp.float32)
        scores = jnp.einsum("qhe,khe->hqk", query_part, key_part) * (HD ** -0.5)
        masked = jnp.where(frame_mask[None], scores, NEG_LARGE)
        row_max = jnp.max(masked, axis=2, keepdims=True)
        weights = jnp.where(frame_mask[None], jnp.exp(masked - row_max), 0.0)
        row_total = jnp.sum(weights, axis=2)
        rounded = lax.optimization_barrier(weights.astype(jnp.bfloat16)).astype(jnp.float32)
        context = jnp.einsum("hqk,khe->qhe", rounded, value_part) / jnp.transpose(row_total)[:, :, None]
        return context.reshape(FR_DEV, D).astype(jnp.bfloat16)

    shards = lax.map(one_shard, jnp.arange(N_SEQ, dtype=jnp.int32))
    return shards.reshape(FRAMES, D)
```

```python
import functools

import jax
import jax.numpy as jnp
from jax import lax
from jax.experimental import pallas as pl
from jax.experimental.pallas import tpu as pltpu
from jax.sharding import PartitionSpec as P

HD = 64
LOOK = 3
NEG_LARGE = -1e30
MESH = pl.DeviceIdType.MESH


def dot(a, b):
    return jnp.dot(a, b, preferred_element_type=jnp.float32)


def dot_t(a, b):
    return lax.dot_general(a, b, (((1,), (1,)), ((), ())), preferred_element_type=jnp.float32)


def kernel(
    n, inside,
    bank_row, lang_ids, seg_ids, lookback, frames, w_query, w_key, w_value, down, up,
    out,
    x, wq, wk, wv, d_mine, u_mine, d_bank, u_bank, d_send, u_send, q_two, acc, top, tot,
    local_sem, f_send, f_recv, t_send, t_recv, a_send, a_recv, dt_send, dt_recv,
):
    me = lax.axis_index("seq")
    h = lax.axis_index("head")
    rows, half = frames.shape
    columns = w_query.shape[1]
    pairs = columns // 128

    def local(src, dst, i):
        return pltpu.make_async_copy(src, dst, local_sem.at[i])

    own = local(frames, x.at[0, h], 0)
    own.start()
    if inside:
        bank_d = local(down, d_bank, 4)
        bank_u = local(up, u_bank, 5)
    else:
        bank_d = local(down, d_mine, 4)
        bank_u = local(up, u_mine, 5)
    bank_d.start()
    bank_u.start()
    weights = [local(w_query, wq, 1), local(w_key, wk, 2), local(w_value, wv, 3)]
    for c in weights:
        c.start()

    barrier = pltpu.get_barrier_semaphore()
    twin = {"head": 1 - h}
    if inside:
        steps = list(range(1, n))
    else:
        steps = [1, 2, 3, n - 3, n - 2, n - 1]
    pl.semaphore_signal(barrier, inc=1, device_id=twin, device_id_type=MESH)
    for k in steps:
        pl.semaphore_signal(barrier, inc=1, device_id={"seq": lax.rem(me + k, n)}, device_id_type=MESH)
    pl.semaphore_wait(barrier, len(steps) + 1)

    def frame_copy(d):
        return pltpu.make_async_remote_copy(
            src_ref=frames, dst_ref=x.at[d, h], send_sem=f_send.at[d - 1], recv_sem=f_recv.at[d - 1],
            device_id={"seq": lax.rem(me + d, n)}, device_id_type=MESH)

    def twin_copy(d):
        return pltpu.make_async_remote_copy(
            src_ref=frames if d == 0 else x.at[d, h], dst_ref=x.at[d, h],
            send_sem=t_send.at[d], recv_sem=t_recv.at[d], device_id=twin, device_id_type=MESH)

    twin_copy(0).start()

    def adapter_copies(k):
        to = {"seq": lax.rem(me + k, n)}
        return (
            pltpu.make_async_remote_copy(
                src_ref=d_send.at[k - 1], dst_ref=d_mine.at[me, h], send_sem=a_send.at[0, k - 1],
                recv_sem=a_recv.at[0, k - 1], device_id=to, device_id_type=MESH),
            pltpu.make_async_remote_copy(
                src_ref=u_send.at[k - 1], dst_ref=u_mine.at[me], send_sem=a_send.at[1, k - 1],
                recv_sem=a_recv.at[1, k - 1], device_id=to, device_id_type=MESH))

    def adapter_arrivals(k):
        source = lax.rem(me + n - k, n)
        return (
            pltpu.make_async_remote_copy(
                src_ref=d_send.at[k - 1], dst_ref=d_mine.at[source, h], send_sem=a_send.at[0, k - 1],
                recv_sem=a_recv.at[0, k - 1], device_id=twin, device_id_type=MESH),
            pltpu.make_async_remote_copy(
                src_ref=u_send.at[k - 1], dst_ref=u_mine.at[source], send_sem=a_send.at[1, k - 1],
                recv_sem=a_recv.at[1, k - 1], device_id=twin, device_id_type=MESH))

    if inside:
        piece = d_send.shape[1]
        first = pl.multiple_of(h * piece, piece)
        bank_d.wait()
        bank_u.wait()
        for k in range(1, n):
            row = bank_row[lang_ids[lax.rem(me + k, n)]]
            d_send[k - 1] = d_bank[row, pl.ds(first, piece), :]
            u_send[k - 1] = u_bank[row]
            for c in adapter_copies(k):
                c.start()
        row = bank_row[lang_ids[me]]
        d_mine[me, h] = d_bank[row, pl.ds(first, piece), :]
        u_mine[me] = u_bank[row]

    for d in range(1, LOOK + 1):
        @pl.when(me + d < n)
        def _():
            frame_copy(d).start()

    lane = lax.broadcasted_iota(jnp.int32, (rows, 128), 1)
    low = lane < HD

    own.wait()
    twin_copy(0).wait_recv()
    for c in weights:
        c.wait()

    def project(d, w):
        return dot(x[d, 0], w[:half]) + dot(x[d, 1], w[half:])

    q = (project(0, wq).astype(jnp.bfloat16).astype(jnp.float32) * HD ** (-0.5)).astype(jnp.bfloat16)
    for j in range(pairs):
        part = q[:, j * 128:(j + 1) * 128]
        q_two[0, :, j * 128:(j + 1) * 128] = jnp.where(low, part, jnp.zeros_like(part))
        q_two[1, :, j * 128:(j + 1) * 128] = jnp.where(low, jnp.zeros_like(part), part)

    if inside:
        for k in range(1, n):
            for c in adapter_arrivals(k):
                c.wait_recv()
        d_hand = pltpu.make_async_remote_copy(
            src_ref=d_mine.at[:, h], dst_ref=d_mine.at[:, h], send_sem=dt_send, recv_sem=dt_recv,
            device_id=twin, device_id_type=MESH)
        d_hand.start()
        d_hand.wait_recv()
    else:
        bank_d.wait()
        bank_u.wait()

    def hand_over(d):
        @pl.when(me >= d)
        def _():
            frame_copy(d).wait_recv()
            twin_copy(d).start()

        @pl.when(me < d)
        def _():
            x[d] = jnp.zeros(x.shape[1:], x.dtype)

    def arrived(d):
        @pl.when(me >= d)
        def _():
            twin_copy(d).wait_recv()

    def keys_values(d):
        flat_d = d_mine[...].reshape(2 * half, 128)
        flat_u = u_mine[...].reshape(128, columns)
        low_rank = (dot(x[d, 0], flat_d[:half]) + dot(x[d, 1], flat_d[half:])).astype(jnp.bfloat16)
        none = jnp.zeros_like(low_rank)
        key = (project(d, wk) + dot(jnp.where(low, low_rank, none), flat_u)).astype(jnp.bfloat16)
        value = (project(d, wv) + dot(jnp.where(low, none, low_rank), flat_u)).astype(jnp.bfloat16)
        return key, value

    def attend(d):
        key, value = keys_values(d)
        if d > 0:
            behind = jnp.maximum(me - d, 0)
            allowed = (me >= d) & (lookback[me] >= d) & (seg_ids[behind] == seg_ids[me])
            bias = jnp.where(allowed, 0.0, NEG_LARGE).astype(jnp.float32)
        for j in range(pairs):
            cols = slice(j * 128, (j + 1) * 128)
            outs, factors = [], []
            for e in range(2):
                head = 2 * j + e
                s = dot_t(q_two[e, :, cols], key[:, cols])
                if d == 0:
                    m = jnp.max(s, axis=1, keepdims=True)
                    w = jnp.exp(s - m)
                    total = jnp.sum(w, axis=1, keepdims=True)
                else:
                    s = s + bias
                    before = top[head][:, :1]
                    m = jnp.maximum(before, jnp.max(s, axis=1, keepdims=True))
                    w = jnp.exp(s - m)
                    factor = jnp.exp(before - m)
                    total = tot[head][:, :1] * factor + jnp.sum(w, axis=1, keepdims=True)
                    factors.append(factor)
                top[head] = jnp.broadcast_to(m, (rows, 128))
                tot[head] = jnp.broadcast_to(total, (rows, 128))
                outs.append(dot(w.astype(jnp.bfloat16), value[:, cols]))
            new = jnp.where(low, outs[0], outs[1])
            if d > 0:
                new = new + acc[:, cols] * jnp.where(low, factors[0], factors[1])
            if d == LOOK:
                new = new / jnp.where(low, tot[2 * j], tot[2 * j + 1])
                out[:, cols] = new.astype(out.dtype)
            else:
                acc[:, cols] = new

    attend(0)
    for d in range(1, LOOK + 1):
        hand_over(d)
        arrived(d)
        attend(d)

    for d in range(LOOK + 1):
        if d == 0:
            twin_copy(0).wait_send()
        else:
            @pl.when(me >= d)
            def _():
                twin_copy(d).wait_send()

            @pl.when(me + d < n)
            def _():
                frame_copy(d).wait_send()
    if inside:
        for k in range(1, n):
            for c in adapter_copies(k):
                c.wait_send()
        d_hand.wait_send()


def body(frames, w_query, w_key, w_value, down_bank, up_bank, bank_row, lang_ids, seg_ids, lookback):
    n = lax.axis_size("seq")
    rows, half = frames.shape
    columns = w_query.shape[1]
    bank_rows, d_rows, rank_two = down_bank.shape
    u_rows = up_bank.shape[1]
    inside = d_rows % 32 == 0 and u_rows % 16 == 0
    bf16, f32 = jnp.bfloat16, jnp.float32
    if inside:
        down, up = down_bank, up_bank
        d_shape, u_shape = (n, 2, d_rows // 2, rank_two), (n, u_rows, columns)
        banks = [down_bank.shape, up_bank.shape, (n - 1, d_rows // 2, rank_two), (n - 1, u_rows, columns)]
    else:
        wanted = jnp.take(bank_row, lang_ids, axis=0)
        down = lax.all_to_all(jnp.take(down_bank, wanted, axis=0), "seq", split_axis=0, concat_axis=1, tiled=True)
        up = lax.all_to_all(jnp.take(up_bank, wanted, axis=0), "seq", split_axis=0, concat_axis=1, tiled=True)
        down, up = down.reshape(d_rows * n, rank_two), up.reshape(u_rows * n, columns)
        d_shape, u_shape = down.shape, up.shape
        banks = [(16, 128)] * 4
    steps = n - 1 if inside else 1
    smem = pl.BlockSpec(memory_space=pltpu.SMEM)
    anywhere = pl.BlockSpec(memory_space=pl.ANY)
    dma = pltpu.SemaphoreType.DMA
    return pl.pallas_call(
        functools.partial(kernel, n, inside),
        out_shape=jax.ShapeDtypeStruct((rows, columns), bf16),
        in_specs=[smem] * 4 + [anywhere] * 6,
        out_specs=pl.BlockSpec(memory_space=pltpu.VMEM),
        scratch_shapes=[
            pltpu.VMEM((LOOK + 1, 2, rows, half), bf16),
            *[pltpu.VMEM(w_query.shape, bf16)] * 3,
            pltpu.VMEM(d_shape, bf16),
            pltpu.VMEM(u_shape, bf16),
            *[pltpu.VMEM(s, bf16) for s in banks],
            pltpu.VMEM((2, rows, columns), bf16),
            pltpu.VMEM((rows, columns), f32),
            *[pltpu.VMEM((columns // HD, rows, 128), f32)] * 2,
            dma((6,)), dma((LOOK,)), dma((LOOK,)), dma((LOOK + 1,)), dma((LOOK + 1,)),
            dma((2, steps)), dma((2, steps)), dma, dma,
        ],
        compiler_params=pltpu.CompilerParams(
            collective_id=0, has_side_effects=True, vmem_limit_bytes=50 * 2 ** 20),
        cost_estimate=pl.CostEstimate(flops=6 * 10 ** 9, bytes_accessed=8 * 2 ** 20, transcendentals=2 ** 21),
    )(bank_row, lang_ids, seg_ids, lookback, frames, w_query, w_key, w_value, down, up)


def solution(mesh):
    in_specs = (
        P(("parts", "seq"), "head"),
        P(None, "head"),
        P(None, "head"),
        P(None, "head"),
        P(None, "seq", None),
        P(None, "seq", "head"),
        P(),
        P("parts"),
        P("parts"),
        P("parts"),
    )
    out_specs = P(("parts", "seq"), "head")
    return jax.shard_map(body, mesh=mesh, in_specs=in_specs, out_specs=out_specs, check_vma=False)
```

```python
import functools

import jax
import jax.numpy as jnp
from jax import lax
from jax.experimental import pallas as pl
from jax.experimental.pallas import tpu as pltpu
from jax.sharding import PartitionSpec as P

HD = 64
LOOK = 3
NEG_LARGE = -1e30
MESH = pl.DeviceIdType.MESH


def dot(a, b):
    return jnp.dot(a, b, preferred_element_type=jnp.float32)


def dot_t(a, b):
    return lax.dot_general(a, b, (((1,), (1,)), ((), ())), preferred_element_type=jnp.float32)


def kernel(
    n,
    bank_row_any, lang_any, seg_any, look_any, frames, w_query, w_key, w_value, down, up,
    out,
    bank_row, lang_ids, seg_ids, lookback,
    x, wq, wk, wv, d_mine, u_mine, d_bank, u_bank, d_send, u_send, q_two, acc, top, tot,
    local_sem, f_send, f_recv, t_send, t_recv, a_send, a_recv, dt_send, dt_recv,
):
    me = lax.axis_index("seq")
    h = lax.axis_index("head")
    rows, half = frames.shape
    columns = w_query.shape[1]
    pairs = columns // 128

    def local(src, dst, i):
        return pltpu.make_async_copy(src, dst, local_sem.at[i])

    own = local(frames, x.at[0, h], 0)
    tables = [
        local(bank_row_any, bank_row, 6), local(lang_any, lang_ids, 7),
        local(seg_any, seg_ids, 8), local(look_any, lookback, 9)]
    for c in tables:
        c.start()
    own.start()
    bank_d = local(down, d_bank, 4)
    bank_u = local(up, u_bank, 5)
    bank_d.start()
    bank_u.start()
    weights = [local(w_query, wq, 1), local(w_key, wk, 2), local(w_value, wv, 3)]
    for c in weights:
        c.start()

    barrier = pltpu.get_barrier_semaphore()
    twin = {"head": 1 - h}
    steps = range(1, n)
    pl.semaphore_signal(barrier, inc=1, device_id=twin, device_id_type=MESH)
    for k in steps:
        pl.semaphore_signal(barrier, inc=1, device_id={"seq": lax.rem(me + k, n)}, device_id_type=MESH)
    pl.semaphore_wait(barrier, len(steps) + 1)

    def frame_copy(d):
        return pltpu.make_async_remote_copy(
            src_ref=frames, dst_ref=x.at[d, h], send_sem=f_send.at[d - 1], recv_sem=f_recv.at[d - 1],
            device_id={"seq": lax.rem(me + d, n)}, device_id_type=MESH)

    def twin_copy(d):
        return pltpu.make_async_remote_copy(
            src_ref=frames if d == 0 else x.at[d, h], dst_ref=x.at[d, h],
            send_sem=t_send.at[d], recv_sem=t_recv.at[d], device_id=twin, device_id_type=MESH)

    twin_copy(0).start()
    for c in tables:
        c.wait()

    def adapter_copies(k):
        to = {"seq": lax.rem(me + k, n)}
        return (
            pltpu.make_async_remote_copy(
                src_ref=d_send.at[k - 1], dst_ref=d_mine.at[me, h], send_sem=a_send.at[0, k - 1],
                recv_sem=a_recv.at[0, k - 1], device_id=to, device_id_type=MESH),
            pltpu.make_async_remote_copy(
                src_ref=u_send.at[k - 1], dst_ref=u_mine.at[me], send_sem=a_send.at[1, k - 1],
                recv_sem=a_recv.at[1, k - 1], device_id=to, device_id_type=MESH))

    def adapter_arrivals(k):
        source = lax.rem(me + n - k, n)
        return (
            pltpu.make_async_remote_copy(
                src_ref=d_send.at[k - 1], dst_ref=d_mine.at[source, h], send_sem=a_send.at[0, k - 1],
                recv_sem=a_recv.at[0, k - 1], device_id=twin, device_id_type=MESH),
            pltpu.make_async_remote_copy(
                src_ref=u_send.at[k - 1], dst_ref=u_mine.at[source], send_sem=a_send.at[1, k - 1],
                recv_sem=a_recv.at[1, k - 1], device_id=twin, device_id_type=MESH))

    piece = d_send.shape[1]
    first = pl.multiple_of(h * piece, piece)
    bank_d.wait()
    bank_u.wait()
    for k in range(1, n):
        row = bank_row[lang_ids[lax.rem(me + k, n)]]
        d_send[k - 1] = d_bank[row, pl.ds(first, piece), :]
        u_send[k - 1] = u_bank[row]
        for c in adapter_copies(k):
            c.start()
    row = bank_row[lang_ids[me]]
    d_mine[me, h] = d_bank[row, pl.ds(first, piece), :]
    u_mine[me] = u_bank[row]

    for d in range(1, LOOK + 1):
        @pl.when(me + d < n)
        def _():
            frame_copy(d).start()

    lane = lax.broadcasted_iota(jnp.int32, (rows, 128), 1)
    low = lane < HD

    own.wait()
    twin_copy(0).wait_recv()
    for c in weights:
        c.wait()

    def project(d, w):
        return dot(x[d, 0], w[:half]) + dot(x[d, 1], w[half:])

    q = (project(0, wq).astype(jnp.bfloat16).astype(jnp.float32) * HD ** (-0.5)).astype(jnp.bfloat16)
    for j in range(pairs):
        part = q[:, j * 128:(j + 1) * 128]
        q_two[0, :, j * 128:(j + 1) * 128] = jnp.where(low, part, jnp.zeros_like(part))
        q_two[1, :, j * 128:(j + 1) * 128] = jnp.where(low, jnp.zeros_like(part), part)

    for k in range(1, n):
        for c in adapter_arrivals(k):
            c.wait_recv()
    d_hand = pltpu.make_async_remote_copy(
        src_ref=d_mine.at[:, h], dst_ref=d_mine.at[:, h], send_sem=dt_send, recv_sem=dt_recv,
        device_id=twin, device_id_type=MESH)
    d_hand.start()
    d_hand.wait_recv()

    def hand_over(d):
        @pl.when(me >= d)
        def _():
            frame_copy(d).wait_recv()
            twin_copy(d).start()

        @pl.when(me < d)
        def _():
            x[d] = jnp.zeros(x.shape[1:], x.dtype)

    def arrived(d):
        @pl.when(me >= d)
        def _():
            twin_copy(d).wait_recv()

    def keys_values(d):
        flat_d = d_mine[...].reshape(2 * half, 128)
        flat_u = u_mine[...].reshape(128, columns)
        low_rank = (dot(x[d, 0], flat_d[:half]) + dot(x[d, 1], flat_d[half:])).astype(jnp.bfloat16)
        none = jnp.zeros_like(low_rank)
        key = (project(d, wk) + dot(jnp.where(low, low_rank, none), flat_u)).astype(jnp.bfloat16)
        value = (project(d, wv) + dot(jnp.where(low, none, low_rank), flat_u)).astype(jnp.bfloat16)
        return key, value

    def attend(d):
        key, value = keys_values(d)
        if d > 0:
            behind = jnp.maximum(me - d, 0)
            allowed = (me >= d) & (lookback[me] >= d) & (seg_ids[behind] == seg_ids[me])
            bias = jnp.where(allowed, 0.0, NEG_LARGE).astype(jnp.float32)
        for j in range(pairs):
            cols = slice(j * 128, (j + 1) * 128)
            outs, factors = [], []
            for e in range(2):
                head = 2 * j + e
                s = dot_t(q_two[e, :, cols], key[:, cols])
                if d == 0:
                    m = jnp.max(s, axis=1, keepdims=True)
                    w = jnp.exp(s - m)
                    total = jnp.sum(w, axis=1, keepdims=True)
                else:
                    s = s + bias
                    before = top[head][:, :1]
                    m = jnp.maximum(before, jnp.max(s, axis=1, keepdims=True))
                    w = jnp.exp(s - m)
                    factor = jnp.exp(before - m)
                    total = tot[head][:, :1] * factor + jnp.sum(w, axis=1, keepdims=True)
                    factors.append(factor)
                top[head] = jnp.broadcast_to(m, (rows, 128))
                tot[head] = jnp.broadcast_to(total, (rows, 128))
                outs.append(dot(w.astype(jnp.bfloat16), value[:, cols]))
            new = jnp.where(low, outs[0], outs[1])
            if d > 0:
                new = new + acc[:, cols] * jnp.where(low, factors[0], factors[1])
            if d == LOOK:
                new = new / jnp.where(low, tot[2 * j], tot[2 * j + 1])
                out[:, cols] = new.astype(out.dtype)
            else:
                acc[:, cols] = new

    attend(0)
    for d in range(1, LOOK + 1):
        hand_over(d)
        arrived(d)
        attend(d)

    for d in range(LOOK + 1):
        if d == 0:
            twin_copy(0).wait_send()
        else:
            @pl.when(me >= d)
            def _():
                twin_copy(d).wait_send()

            @pl.when(me + d < n)
            def _():
                frame_copy(d).wait_send()
    for k in range(1, n):
        for c in adapter_copies(k):
            c.wait_send()
    d_hand.wait_send()


def from_behind(block, axis, distance):
    devices = range(lax.axis_size(axis))
    route = [(i - distance, i) for i in devices if i - distance in devices]
    return lax.ppermute(block, axis, route)


def block_rules(seg_ids, lookback, position, distance, blocks_dev, block_len):
    query_first = position * blocks_dev
    key_first = (position - distance) * blocks_dev
    counter = jnp.arange(blocks_dev, dtype=jnp.int32)
    query_blocks = query_first + counter
    key_blocks = key_first + counter
    query_seg = lax.dynamic_slice_in_dim(seg_ids, query_first, blocks_dev)
    query_reach = lax.dynamic_slice_in_dim(lookback, query_first, blocks_dev)
    key_seg = lax.dynamic_slice_in_dim(seg_ids, jnp.maximum(key_first, 0), blocks_dev)
    allowed = key_blocks[None, :] >= query_blocks[:, None] - query_reach[:, None]
    allowed = allowed & (key_blocks[None, :] <= query_blocks[:, None])
    allowed = allowed & (key_seg[None, :] == query_seg[:, None]) & (key_blocks[None, :] >= 0)
    frames_dev = blocks_dev * block_len
    expanded = jnp.broadcast_to(
        allowed[:, None, :, None], (blocks_dev, block_len, blocks_dev, block_len)
    )
    return (jnp.any(allowed), expanded.reshape(frames_dev, frames_dev))


def attend(carried, query_heads, pair, allowed):
    run_max, run_sum, run_acc = carried
    frames_dev = query_heads.shape[0]
    heads_dev = query_heads.shape[1]
    key_heads = pair[0].reshape(frames_dev, heads_dev, HD)
    value_heads = pair[1].reshape(frames_dev, heads_dev, HD)
    scores = jnp.einsum(
        "qhe,khe->hqk", query_heads, key_heads, preferred_element_type=jnp.float32
    ) * HD ** (-0.5)
    masked = jnp.where(allowed[None], scores, NEG_LARGE)
    new_max = jnp.maximum(run_max, jnp.max(masked, axis=2))
    factor = jnp.exp(run_max - new_max)
    weights = jnp.where(allowed[None], jnp.exp(masked - new_max[:, :, None]), 0.0)
    new_sum = run_sum * factor + jnp.sum(weights, axis=2)
    update = jnp.einsum(
        "hqk,khe->hqe",
        weights.astype(jnp.bfloat16),
        value_heads,
        preferred_element_type=jnp.float32,
    )
    return (new_max, new_sum, run_acc * factor[:, :, None] + update)


def plain_body(
    frames, w_query, w_key, w_value, down_bank, up_bank, bank_row, lang_ids, seg_ids, lookback
):
    seq_count = lax.axis_size("seq")
    position = lax.axis_index("seq")
    frames_dev = frames.shape[0]
    blocks_dev = lang_ids.shape[0] // seq_count
    block_len = frames_dev // blocks_dev
    model_width = w_query.shape[0]
    columns = w_query.shape[1]
    heads_dev = columns // HD
    rank_two = down_bank.shape[2]
    rank_half = rank_two // 2
    wanted = jnp.transpose(jnp.take(bank_row, lang_ids, axis=0).reshape(seq_count, blocks_dev))
    picked = (wanted[:, :, None] == jnp.arange(down_bank.shape[0])).astype(jnp.bfloat16)
    down_send = jnp.einsum("wbl,lrc->wbrc", picked, down_bank)
    up_send = jnp.einsum("wbl,lrc->wbrc", picked, up_bank)
    down_got, up_got = (
        lax.all_to_all(down_send, "seq", split_axis=1, concat_axis=2, tiled=True),
        lax.all_to_all(up_send, "seq", split_axis=1, concat_axis=2, tiled=True),
    )
    down_mine = down_got.reshape(blocks_dev, model_width, rank_two)
    up_mine = up_got.reshape(blocks_dev, rank_two, columns)
    gathered = lax.all_gather(frames, "head", axis=1, tiled=True)
    queries = jnp.dot(gathered, w_query, preferred_element_type=jnp.float32).astype(jnp.bfloat16)
    block_rows = gathered.reshape(blocks_dev, block_len, model_width)
    lowrank = jnp.einsum(
        "bfd,bdr->bfr", block_rows, down_mine, preferred_element_type=jnp.float32
    ).astype(jnp.bfloat16)
    key_extra = jnp.einsum(
        "bfr,brc->bfc",
        lowrank[:, :, :rank_half],
        up_mine[:, :rank_half],
        preferred_element_type=jnp.float32,
    )
    value_extra = jnp.einsum(
        "bfr,brc->bfc",
        lowrank[:, :, rank_half:],
        up_mine[:, rank_half:],
        preferred_element_type=jnp.float32,
    )
    own_keys = (
        jnp.dot(gathered, w_key, preferred_element_type=jnp.float32)
        + key_extra.reshape(frames_dev, columns)
    ).astype(jnp.bfloat16)
    own_values = (
        jnp.dot(gathered, w_value, preferred_element_type=jnp.float32)
        + value_extra.reshape(frames_dev, columns)
    ).astype(jnp.bfloat16)
    own_pair = jnp.stack([own_keys, own_values])
    query_heads = queries.reshape(frames_dev, heads_dev, HD)
    initial = (
        jnp.full((heads_dev, frames_dev), NEG_LARGE, jnp.float32),
        jnp.zeros((heads_dev, frames_dev), jnp.float32),
        jnp.zeros((heads_dev, frames_dev, HD), jnp.float32),
    )

    def visit_tile(carried, pair, distance):
        nonempty, allowed = block_rules(
            seg_ids, lookback, position, distance, blocks_dev, block_len
        )
        return attend(carried, query_heads, pair, allowed)

    carried = visit_tile(initial, own_pair, 0)
    moving = own_pair
    for distance in range(1, 4):
        moving = from_behind(moving, "seq", 1)
        carried = visit_tile(carried, moving, distance)
    run_max, run_sum, run_acc = carried
    context = (run_acc / run_sum[:, :, None]).astype(jnp.bfloat16)
    return jnp.transpose(context, (1, 0, 2)).reshape(frames_dev, columns)


def body(frames, w_query, w_key, w_value, down_bank, up_bank, bank_row, lang_ids, seg_ids, lookback):
    n = lax.axis_size("seq")
    rows, half = frames.shape
    columns = w_query.shape[1]
    bank_rows, d_rows, rank_two = down_bank.shape
    u_rows = up_bank.shape[1]
    if d_rows % 32 or u_rows % 16 or lang_ids.shape[0] != n:
        return plain_body(
            frames, w_query, w_key, w_value, down_bank, up_bank, bank_row, lang_ids, seg_ids, lookback)
    bf16, f32 = jnp.bfloat16, jnp.float32
    d_shape, u_shape = (n, 2, d_rows // 2, rank_two), (n, u_rows, columns)
    banks = [down_bank.shape, up_bank.shape, (n - 1, d_rows // 2, rank_two), (n - 1, u_rows, columns)]
    hbm = pl.BlockSpec(memory_space=pltpu.HBM)
    dma = pltpu.SemaphoreType.DMA
    return pl.pallas_call(
        functools.partial(kernel, n),
        out_shape=jax.ShapeDtypeStruct((rows, columns), bf16),
        in_specs=[hbm] * 10,
        out_specs=pl.BlockSpec(memory_space=pltpu.VMEM),
        scratch_shapes=[
            *[pltpu.SMEM(t.shape, jnp.int32) for t in (bank_row, lang_ids, seg_ids, lookback)],
            pltpu.VMEM((LOOK + 1, 2, rows, half), bf16),
            *[pltpu.VMEM(w_query.shape, bf16)] * 3,
            pltpu.VMEM(d_shape, bf16),
            pltpu.VMEM(u_shape, bf16),
            *[pltpu.VMEM(s, bf16) for s in banks],
            pltpu.VMEM((2, rows, columns), bf16),
            pltpu.VMEM((rows, columns), f32),
            *[pltpu.VMEM((columns // HD, rows, 128), f32)] * 2,
            dma((10,)), dma((LOOK,)), dma((LOOK,)), dma((LOOK + 1,)), dma((LOOK + 1,)),
            dma((2, n - 1)), dma((2, n - 1)), dma, dma,
        ],
        compiler_params=pltpu.CompilerParams(
            collective_id=0, has_side_effects=True, vmem_limit_bytes=60 * 2 ** 20),
        cost_estimate=pl.CostEstimate(flops=6 * 10 ** 9, bytes_accessed=8 * 2 ** 20, transcendentals=2 ** 21),
    )(bank_row, lang_ids, seg_ids, lookback, frames, w_query, w_key, w_value, down_bank, up_bank)


def solution(mesh):
    in_specs = (
        P(("parts", "seq"), "head"),
        P(None, "head"),
        P(None, "head"),
        P(None, "head"),
        P(None, "seq", None),
        P(None, "seq", "head"),
        P(),
        P("parts"),
        P("parts"),
        P("parts"),
    )
    out_specs = P(("parts", "seq"), "head")
    return jax.shard_map(body, mesh=mesh, in_specs=in_specs, out_specs=out_specs, check_vma=False)
```

```python
import functools

import jax
import jax.numpy as jnp
from jax import lax
from jax.experimental import pallas as pl
from jax.experimental.pallas import tpu as pltpu
from jax.sharding import PartitionSpec as P

HD = 64
LOOK = 3
CHUNKS = 2
NEG_LARGE = -1e30
MESH = pl.DeviceIdType.MESH


def dot(a, b):
    return jnp.dot(a, b, preferred_element_type=jnp.float32)


def dot_t(a, b):
    return lax.dot_general(a, b, (((1,), (1,)), ((), ())), preferred_element_type=jnp.float32)


def kernel(
    n,
    bank_row_any, lang_any, seg_any, look_any, frames, w_query, w_key, w_value, down, up,
    out,
    bank_row, lang_ids, seg_ids, lookback,
    x, wq, wk, wv, d_mine, u_mine, d_bank, u_bank, d_send, u_send, q_two, acc, top, tot,
    local_sem, f_send, f_recv, t_send, t_recv, a_send, a_recv, dt_send, dt_recv,
):
    me = lax.axis_index("seq")
    h = lax.axis_index("head")
    rows, half = frames.shape
    columns = w_query.shape[1]
    pairs = columns // 128

    def local(src, dst, i):
        return pltpu.make_async_copy(src, dst, local_sem.at[i])

    own = local(frames, x.at[0, h], 0)
    tables = [
        local(bank_row_any, bank_row, 6), local(lang_any, lang_ids, 7),
        local(seg_any, seg_ids, 8), local(look_any, lookback, 9)]
    for c in tables:
        c.start()
    own.start()
    bank_d = local(down, d_bank, 4)
    bank_u = local(up, u_bank, 5)
    bank_d.start()
    bank_u.start()
    weights = [local(w_query, wq, 1), local(w_key, wk, 2), local(w_value, wv, 3)]
    for c in weights:
        c.start()

    barrier = pltpu.get_barrier_semaphore()
    twin = {"head": 1 - h}
    steps = range(1, n)
    pl.semaphore_signal(barrier, inc=1, device_id=twin, device_id_type=MESH)
    for k in steps:
        pl.semaphore_signal(barrier, inc=1, device_id={"seq": lax.rem(me + k, n)}, device_id_type=MESH)
    pl.semaphore_wait(barrier, len(steps) + 1)

    even = lax.rem(me, 2) == 0
    size = rows // CHUNKS

    def frame_copy(kind, c, slot, source, to):
        part = pl.ds(c * size, size)
        return pltpu.make_async_remote_copy(
            src_ref=frames.at[part] if source == 0 else x.at[source, h, part],
            dst_ref=x.at[slot, h, part], send_sem=f_send.at[kind, c], recv_sem=f_recv.at[slot - 1, c],
            device_id={"seq": lax.rem(me + to + n, n)}, device_id_type=MESH)

    def twin_copy(d, c=0):
        part = pl.ds(c * size, size) if d else pl.ds(0, rows)
        return pltpu.make_async_remote_copy(
            src_ref=x.at[d, h, part] if d else frames, dst_ref=x.at[d, h, part],
            send_sem=t_send.at[d, c], recv_sem=t_recv.at[d, c], device_id=twin, device_id_type=MESH)

    for c in range(CHUNKS):
        @pl.when(me + 2 < n)
        def _():
            frame_copy(0, c, 2, 0, 2).start()

        @pl.when(even)
        def _():
            frame_copy(1, c, 1, 0, 1).start()

    twin_copy(0).start()
    for c in tables:
        c.wait()

    def adapter_copies(k):
        to = {"seq": lax.rem(me + k, n)}
        return (
            pltpu.make_async_remote_copy(
                src_ref=d_send.at[k - 1], dst_ref=d_mine.at[me, h], send_sem=a_send.at[0, k - 1],
                recv_sem=a_recv.at[0, k - 1], device_id=to, device_id_type=MESH),
            pltpu.make_async_remote_copy(
                src_ref=u_send.at[k - 1], dst_ref=u_mine.at[me], send_sem=a_send.at[1, k - 1],
                recv_sem=a_recv.at[1, k - 1], device_id=to, device_id_type=MESH))

    def adapter_arrivals(k):
        source = lax.rem(me + n - k, n)
        return (
            pltpu.make_async_remote_copy(
                src_ref=d_send.at[k - 1], dst_ref=d_mine.at[source, h], send_sem=a_send.at[0, k - 1],
                recv_sem=a_recv.at[0, k - 1], device_id=twin, device_id_type=MESH),
            pltpu.make_async_remote_copy(
                src_ref=u_send.at[k - 1], dst_ref=u_mine.at[source], send_sem=a_send.at[1, k - 1],
                recv_sem=a_recv.at[1, k - 1], device_id=twin, device_id_type=MESH))

    piece = d_send.shape[1]
    first = pl.multiple_of(h * piece, piece)
    bank_d.wait()
    bank_u.wait()
    for k in range(1, n):
        row = bank_row[lang_ids[lax.rem(me + k, n)]]
        d_send[k - 1] = d_bank[row, pl.ds(first, piece), :]
        u_send[k - 1] = u_bank[row]
        for c in adapter_copies(k):
            c.start()
    row = bank_row[lang_ids[me]]
    d_mine[me, h] = d_bank[row, pl.ds(first, piece), :]
    u_mine[me] = u_bank[row]

    lane = lax.broadcasted_iota(jnp.int32, (rows, 128), 1)
    low = lane < HD

    own.wait()
    twin_copy(0).wait_recv()
    for c in weights:
        c.wait()

    def project(d, w):
        return dot(x[d, 0], w[:half]) + dot(x[d, 1], w[half:])

    q = (project(0, wq).astype(jnp.bfloat16).astype(jnp.float32) * HD ** (-0.5)).astype(jnp.bfloat16)
    for j in range(pairs):
        part = q[:, j * 128:(j + 1) * 128]
        q_two[0, :, j * 128:(j + 1) * 128] = jnp.where(low, part, jnp.zeros_like(part))
        q_two[1, :, j * 128:(j + 1) * 128] = jnp.where(low, jnp.zeros_like(part), part)

    def hand_over(d):
        for c in range(CHUNKS):
            @pl.when(me >= d)
            def _():
                frame_copy(0, c, d, 0, 2).wait_recv()

            if d == 2:
                @pl.when(even & (me >= 2))
                def _():
                    frame_copy(2, c, 3, 2, 1).start()

                @pl.when((~even) & (me >= 3))
                def _():
                    frame_copy(2, c, 1, 2, -1).start()
            if d == 1:
                @pl.when(even & (me >= 2) & (me + 2 < n))
                def _():
                    frame_copy(3, c, 3, 1, 2).start()

            @pl.when(me >= d)
            def _():
                twin_copy(d, c).start()

        @pl.when(me < d)
        def _():
            x[d] = jnp.zeros(x.shape[1:], x.dtype)

    def arrived(d):
        for c in range(CHUNKS):
            @pl.when(me >= d)
            def _():
                twin_copy(d, c).wait_recv()

    hand_over(2)
    for k in range(1, n):
        for c in adapter_arrivals(k):
            c.wait_recv()
    d_hand = pltpu.make_async_remote_copy(
        src_ref=d_mine.at[:, h], dst_ref=d_mine.at[:, h], send_sem=dt_send, recv_sem=dt_recv,
        device_id=twin, device_id_type=MESH)
    d_hand.start()
    d_hand.wait_recv()

    def keys_values(d):
        flat_d = d_mine[...].reshape(2 * half, 128)
        flat_u = u_mine[...].reshape(128, columns)
        low_rank = (dot(x[d, 0], flat_d[:half]) + dot(x[d, 1], flat_d[half:])).astype(jnp.bfloat16)
        none = jnp.zeros_like(low_rank)
        key = (project(d, wk) + dot(jnp.where(low, low_rank, none), flat_u)).astype(jnp.bfloat16)
        value = (project(d, wv) + dot(jnp.where(low, none, low_rank), flat_u)).astype(jnp.bfloat16)
        return key, value

    def attend(d):
        key, value = keys_values(d)
        if d > 0:
            behind = jnp.maximum(me - d, 0)
            allowed = (me >= d) & (lookback[me] >= d) & (seg_ids[behind] == seg_ids[me])
            bias = jnp.where(allowed, 0.0, NEG_LARGE).astype(jnp.float32)
        for j in range(pairs):
            cols = slice(j * 128, (j + 1) * 128)
            outs, factors = [], []
            for e in range(2):
                head = 2 * j + e
                s = dot_t(q_two[e, :, cols], key[:, cols])
                if d == 0:
                    m = jnp.max(s, axis=1, keepdims=True)
                    w = jnp.exp(s - m)
                    total = jnp.sum(w, axis=1, keepdims=True)
                else:
                    s = s + bias
                    before = top[head][:, :1]
                    m = jnp.maximum(before, jnp.max(s, axis=1, keepdims=True))
                    w = jnp.exp(s - m)
                    factor = jnp.exp(before - m)
                    total = tot[head][:, :1] * factor + jnp.sum(w, axis=1, keepdims=True)
                    factors.append(factor)
                top[head] = jnp.broadcast_to(m, (rows, 128))
                tot[head] = jnp.broadcast_to(total, (rows, 128))
                outs.append(dot(w.astype(jnp.bfloat16), value[:, cols]))
            new = jnp.where(low, outs[0], outs[1])
            if d > 0:
                new = new + acc[:, cols] * jnp.where(low, factors[0], factors[1])
            if d == LOOK:
                new = new / jnp.where(low, tot[2 * j], tot[2 * j + 1])
                out[:, cols] = new.astype(out.dtype)
            else:
                acc[:, cols] = new

    attend(0)
    hand_over(1)
    arrived(2)
    attend(2)
    arrived(1)
    attend(1)
    hand_over(3)
    arrived(3)
    attend(3)

    twin_copy(0).wait_send()
    for c in range(CHUNKS):
        for d in range(1, LOOK + 1):
            @pl.when(me >= d)
            def _():
                twin_copy(d, c).wait_send()

        @pl.when(me + 2 < n)
        def _():
            frame_copy(0, c, 2, 0, 2).wait_send()

        @pl.when(even)
        def _():
            frame_copy(1, c, 1, 0, 1).wait_send()

        @pl.when(me >= 2)
        def _():
            frame_copy(2, c, 3, 2, 1).wait_send()

        @pl.when(even & (me >= 2) & (me + 2 < n))
        def _():
            frame_copy(3, c, 3, 1, 2).wait_send()
    for k in range(1, n):
        for c in adapter_copies(k):
            c.wait_send()
    d_hand.wait_send()


def from_behind(block, axis, distance):
    devices = range(lax.axis_size(axis))
    route = [(i - distance, i) for i in devices if i - distance in devices]
    return lax.ppermute(block, axis, route)


def block_rules(seg_ids, lookback, position, distance, blocks_dev, block_len):
    query_first = position * blocks_dev
    key_first = (position - distance) * blocks_dev
    counter = jnp.arange(blocks_dev, dtype=jnp.int32)
    query_blocks = query_first + counter
    key_blocks = key_first + counter
    query_seg = lax.dynamic_slice_in_dim(seg_ids, query_first, blocks_dev)
    query_reach = lax.dynamic_slice_in_dim(lookback, query_first, blocks_dev)
    key_seg = lax.dynamic_slice_in_dim(seg_ids, jnp.maximum(key_first, 0), blocks_dev)
    allowed = key_blocks[None, :] >= query_blocks[:, None] - query_reach[:, None]
    allowed = allowed & (key_blocks[None, :] <= query_blocks[:, None])
    allowed = allowed & (key_seg[None, :] == query_seg[:, None]) & (key_blocks[None, :] >= 0)
    frames_dev = blocks_dev * block_len
    expanded = jnp.broadcast_to(
        allowed[:, None, :, None], (blocks_dev, block_len, blocks_dev, block_len)
    )
    return (jnp.any(allowed), expanded.reshape(frames_dev, frames_dev))


def attend(carried, query_heads, pair, allowed):
    run_max, run_sum, run_acc = carried
    frames_dev = query_heads.shape[0]
    heads_dev = query_heads.shape[1]
    key_heads = pair[0].reshape(frames_dev, heads_dev, HD)
    value_heads = pair[1].reshape(frames_dev, heads_dev, HD)
    scores = jnp.einsum(
        "qhe,khe->hqk", query_heads, key_heads, preferred_element_type=jnp.float32
    ) * HD ** (-0.5)
    masked = jnp.where(allowed[None], scores, NEG_LARGE)
    new_max = jnp.maximum(run_max, jnp.max(masked, axis=2))
    factor = jnp.exp(run_max - new_max)
    weights = jnp.where(allowed[None], jnp.exp(masked - new_max[:, :, None]), 0.0)
    new_sum = run_sum * factor + jnp.sum(weights, axis=2)
    update = jnp.einsum(
        "hqk,khe->hqe",
        weights.astype(jnp.bfloat16),
        value_heads,
        preferred_element_type=jnp.float32,
    )
    return (new_max, new_sum, run_acc * factor[:, :, None] + update)


def plain_body(
    frames, w_query, w_key, w_value, down_bank, up_bank, bank_row, lang_ids, seg_ids, lookback
):
    seq_count = lax.axis_size("seq")
    position = lax.axis_index("seq")
    frames_dev = frames.shape[0]
    blocks_dev = lang_ids.shape[0] // seq_count
    block_len = frames_dev // blocks_dev
    model_width = w_query.shape[0]
    columns = w_query.shape[1]
    heads_dev = columns // HD
    rank_two = down_bank.shape[2]
    rank_half = rank_two // 2
    wanted = jnp.transpose(jnp.take(bank_row, lang_ids, axis=0).reshape(seq_count, blocks_dev))
    picked = (wanted[:, :, None] == jnp.arange(down_bank.shape[0])).astype(jnp.bfloat16)
    down_send = jnp.einsum("wbl,lrc->wbrc", picked, down_bank)
    up_send = jnp.einsum("wbl,lrc->wbrc", picked, up_bank)
    down_got, up_got = (
        lax.all_to_all(down_send, "seq", split_axis=1, concat_axis=2, tiled=True),
        lax.all_to_all(up_send, "seq", split_axis=1, concat_axis=2, tiled=True),
    )
    down_mine = down_got.reshape(blocks_dev, model_width, rank_two)
    up_mine = up_got.reshape(blocks_dev, rank_two, columns)
    gathered = lax.all_gather(frames, "head", axis=1, tiled=True)
    queries = jnp.dot(gathered, w_query, preferred_element_type=jnp.float32).astype(jnp.bfloat16)
    block_rows = gathered.reshape(blocks_dev, block_len, model_width)
    lowrank = jnp.einsum(
        "bfd,bdr->bfr", block_rows, down_mine, preferred_element_type=jnp.float32
    ).astype(jnp.bfloat16)
    key_extra = jnp.einsum(
        "bfr,brc->bfc",
        lowrank[:, :, :rank_half],
        up_mine[:, :rank_half],
        preferred_element_type=jnp.float32,
    )
    value_extra = jnp.einsum(
        "bfr,brc->bfc",
        lowrank[:, :, rank_half:],
        up_mine[:, rank_half:],
        preferred_element_type=jnp.float32,
    )
    own_keys = (
        jnp.dot(gathered, w_key, preferred_element_type=jnp.float32)
        + key_extra.reshape(frames_dev, columns)
    ).astype(jnp.bfloat16)
    own_values = (
        jnp.dot(gathered, w_value, preferred_element_type=jnp.float32)
        + value_extra.reshape(frames_dev, columns)
    ).astype(jnp.bfloat16)
    own_pair = jnp.stack([own_keys, own_values])
    query_heads = queries.reshape(frames_dev, heads_dev, HD)
    initial = (
        jnp.full((heads_dev, frames_dev), NEG_LARGE, jnp.float32),
        jnp.zeros((heads_dev, frames_dev), jnp.float32),
        jnp.zeros((heads_dev, frames_dev, HD), jnp.float32),
    )

    def visit_tile(carried, pair, distance):
        nonempty, allowed = block_rules(
            seg_ids, lookback, position, distance, blocks_dev, block_len
        )
        return attend(carried, query_heads, pair, allowed)

    carried = visit_tile(initial, own_pair, 0)
    moving = own_pair
    for distance in range(1, 4):
        moving = from_behind(moving, "seq", 1)
        carried = visit_tile(carried, moving, distance)
    run_max, run_sum, run_acc = carried
    context = (run_acc / run_sum[:, :, None]).astype(jnp.bfloat16)
    return jnp.transpose(context, (1, 0, 2)).reshape(frames_dev, columns)


def body(frames, w_query, w_key, w_value, down_bank, up_bank, bank_row, lang_ids, seg_ids, lookback):
    n = lax.axis_size("seq")
    rows, half = frames.shape
    columns = w_query.shape[1]
    bank_rows, d_rows, rank_two = down_bank.shape
    u_rows = up_bank.shape[1]
    if n % 2 or d_rows % 32 or u_rows % 16 or lang_ids.shape[0] != n:
        return plain_body(
            frames, w_query, w_key, w_value, down_bank, up_bank, bank_row, lang_ids, seg_ids, lookback)
    bf16, f32 = jnp.bfloat16, jnp.float32
    d_shape, u_shape = (n, 2, d_rows // 2, rank_two), (n, u_rows, columns)
    banks = [down_bank.shape, up_bank.shape, (n - 1, d_rows // 2, rank_two), (n - 1, u_rows, columns)]
    hbm = pl.BlockSpec(memory_space=pltpu.HBM)
    dma = pltpu.SemaphoreType.DMA
    return pl.pallas_call(
        functools.partial(kernel, n),
        out_shape=jax.ShapeDtypeStruct((rows, columns), bf16),
        in_specs=[hbm] * 10,
        out_specs=pl.BlockSpec(memory_space=pltpu.VMEM),
        scratch_shapes=[
            *[pltpu.SMEM(t.shape, jnp.int32) for t in (bank_row, lang_ids, seg_ids, lookback)],
            pltpu.VMEM((LOOK + 1, 2, rows, half), bf16),
            *[pltpu.VMEM(w_query.shape, bf16)] * 3,
            pltpu.VMEM(d_shape, bf16),
            pltpu.VMEM(u_shape, bf16),
            *[pltpu.VMEM(s, bf16) for s in banks],
            pltpu.VMEM((2, rows, columns), bf16),
            pltpu.VMEM((rows, columns), f32),
            *[pltpu.VMEM((columns // HD, rows, 128), f32)] * 2,
            dma((10,)), dma((4, CHUNKS)), dma((LOOK, CHUNKS)), *[dma((LOOK + 1, CHUNKS))] * 2,
            dma((2, n - 1)), dma((2, n - 1)), dma, dma,
        ],
        compiler_params=pltpu.CompilerParams(
            collective_id=0, has_side_effects=True, vmem_limit_bytes=60 * 2 ** 20),
        cost_estimate=pl.CostEstimate(flops=6 * 10 ** 9, bytes_accessed=8 * 2 ** 20, transcendentals=2 ** 21),
    )(bank_row, lang_ids, seg_ids, lookback, frames, w_query, w_key, w_value, down_bank, up_bank)


def solution(mesh):
    in_specs = (
        P(("parts", "seq"), "head"),
        P(None, "head"),
        P(None, "head"),
        P(None, "head"),
        P(None, "seq", None),
        P(None, "seq", "head"),
        P(),
        P("parts"),
        P("parts"),
        P("parts"),
    )
    out_specs = P(("parts", "seq"), "head")
    return jax.shard_map(body, mesh=mesh, in_specs=in_specs, out_specs=out_specs, check_vma=False)
```

```python
import functools

import jax
import jax.numpy as jnp
from jax import lax
from jax.experimental import pallas as pl
from jax.experimental.pallas import tpu as pltpu
from jax.sharding import PartitionSpec as P

HD = 64
LOOK = 3
CHUNKS = 2
NEG_LARGE = -1e30
MESH = pl.DeviceIdType.MESH


def dot(a, b):
    return jnp.dot(a, b, preferred_element_type=jnp.float32)


def dot_t(a, b):
    return lax.dot_general(a, b, (((1,), (1,)), ((), ())), preferred_element_type=jnp.float32)


def kernel(
    n,
    bank_row_any, lang_any, seg_any, look_any, frames, w_query, w_key, w_value, down, up,
    out,
    bank_row, lang_ids, seg_ids, lookback,
    x, wq, wk, wv, d_mine, u_mine, d_bank, u_bank, d_send, u_send, q_two, acc, top, tot,
    local_sem, f_send, f_recv, t_send, t_recv, a_send, a_recv, dt_send, dt_recv,
):
    me = lax.axis_index("seq")
    h = lax.axis_index("head")
    rows, half = frames.shape
    columns = w_query.shape[1]
    pairs = columns // 128

    def local(src, dst, i):
        return pltpu.make_async_copy(src, dst, local_sem.at[i])

    own = local(frames, x.at[0, h], 0)
    tables = [
        local(bank_row_any, bank_row, 6), local(lang_any, lang_ids, 7),
        local(seg_any, seg_ids, 8), local(look_any, lookback, 9)]
    for c in tables:
        c.start()
    own.start()
    bank_d = local(down, d_bank, 4)
    bank_u = local(up, u_bank, 5)
    bank_d.start()
    bank_u.start()
    weights = [local(w_query, wq, 1), local(w_key, wk, 2), local(w_value, wv, 3)]
    for c in weights:
        c.start()

    barrier = pltpu.get_barrier_semaphore()
    twin = {"head": 1 - h}
    steps = range(1, n)
    pl.semaphore_signal(barrier, inc=1, device_id=twin, device_id_type=MESH)
    for k in steps:
        pl.semaphore_signal(barrier, inc=1, device_id={"seq": lax.rem(me + k, n)}, device_id_type=MESH)
    pl.semaphore_wait(barrier, len(steps) + 1)

    even = lax.rem(me, 2) == 0
    size = rows // CHUNKS

    def frame_copy(kind, c, slot, source, to):
        part = pl.ds(c * size, size)
        return pltpu.make_async_remote_copy(
            src_ref=frames.at[part] if source == 0 else x.at[source, h, part],
            dst_ref=x.at[slot, h, part], send_sem=f_send.at[kind, c], recv_sem=f_recv.at[slot - 1, c],
            device_id={"seq": lax.rem(me + to + n, n)}, device_id_type=MESH)

    def twin_copy(d, c=0):
        part = pl.ds(c * size, size) if d else pl.ds(0, rows)
        return pltpu.make_async_remote_copy(
            src_ref=x.at[d, h, part] if d else frames, dst_ref=x.at[d, h, part],
            send_sem=t_send.at[d, c], recv_sem=t_recv.at[d, c], device_id=twin, device_id_type=MESH)

    for c in range(CHUNKS):
        @pl.when(me + 2 < n)
        def _():
            frame_copy(0, c, 2, 0, 2).start()

        @pl.when(even)
        def _():
            frame_copy(1, c, 1, 0, 1).start()

    twin_copy(0).start()
    for c in tables:
        c.wait()

    def adapter_copies(k):
        to = {"seq": lax.rem(me + k, n)}
        return (
            pltpu.make_async_remote_copy(
                src_ref=d_send.at[k - 1], dst_ref=d_mine.at[me, h], send_sem=a_send.at[0, k - 1],
                recv_sem=a_recv.at[0, k - 1], device_id=to, device_id_type=MESH),
            pltpu.make_async_remote_copy(
                src_ref=u_send.at[k - 1], dst_ref=u_mine.at[me], send_sem=a_send.at[1, k - 1],
                recv_sem=a_recv.at[1, k - 1], device_id=to, device_id_type=MESH))

    def adapter_arrivals(k):
        source = lax.rem(me + n - k, n)
        return (
            pltpu.make_async_remote_copy(
                src_ref=d_send.at[k - 1], dst_ref=d_mine.at[source, h], send_sem=a_send.at[0, k - 1],
                recv_sem=a_recv.at[0, k - 1], device_id=twin, device_id_type=MESH),
            pltpu.make_async_remote_copy(
                src_ref=u_send.at[k - 1], dst_ref=u_mine.at[source], send_sem=a_send.at[1, k - 1],
                recv_sem=a_recv.at[1, k - 1], device_id=twin, device_id_type=MESH))

    piece = d_send.shape[1]
    first = pl.multiple_of(h * piece, piece)
    bank_d.wait()
    bank_u.wait()
    for k in range(1, n):
        row = bank_row[lang_ids[lax.rem(me + k, n)]]
        d_send[k - 1] = d_bank[row, pl.ds(first, piece), :]
        u_send[k - 1] = u_bank[row]
        for c in adapter_copies(k):
            c.start()
    row = bank_row[lang_ids[me]]
    d_mine[me, h] = d_bank[row, pl.ds(first, piece), :]
    u_mine[me] = u_bank[row]

    lane = lax.broadcasted_iota(jnp.int32, (rows, 128), 1)
    low = lane < HD

    own.wait()
    twin_copy(0).wait_recv()
    for c in weights:
        c.wait()

    def project(d, w):
        return dot(x[d, 0], w[:half]) + dot(x[d, 1], w[half:])

    q = (project(0, wq).astype(jnp.bfloat16).astype(jnp.float32) * HD ** (-0.5)).astype(jnp.bfloat16)
    for j in range(pairs):
        part = q[:, j * 128:(j + 1) * 128]
        q_two[0, :, j * 128:(j + 1) * 128] = jnp.where(low, part, jnp.zeros_like(part))
        q_two[1, :, j * 128:(j + 1) * 128] = jnp.where(low, jnp.zeros_like(part), part)

    def hand_over(d):
        for c in range(CHUNKS):
            @pl.when(me >= d)
            def _():
                frame_copy(0, c, d, 0, 2).wait_recv()

            if d == 2:
                @pl.when(even & (me >= 2))
                def _():
                    frame_copy(2, c, 3, 2, 1).start()

                @pl.when((~even) & (me >= 3))
                def _():
                    frame_copy(2, c, 1, 2, -1).start()
            if d == 1:
                @pl.when(even & (me >= 2) & (me + 2 < n))
                def _():
                    frame_copy(3, c, 3, 1, 2).start()

            @pl.when(me >= d)
            def _():
                twin_copy(d, c).start()

        @pl.when(me < d)
        def _():
            x[d] = jnp.zeros(x.shape[1:], x.dtype)

    def arrived(d):
        for c in range(CHUNKS):
            @pl.when(me >= d)
            def _():
                twin_copy(d, c).wait_recv()

    hand_over(2)
    for k in range(1, n):
        for c in adapter_arrivals(k):
            c.wait_recv()
    d_hand = pltpu.make_async_remote_copy(
        src_ref=d_mine.at[:, h], dst_ref=d_mine.at[:, h], send_sem=dt_send, recv_sem=dt_recv,
        device_id=twin, device_id_type=MESH)
    d_hand.start()
    d_hand.wait_recv()

    def keys_values(d):
        flat_d = d_mine[...].reshape(2 * half, 128)
        flat_u = u_mine[...].reshape(128, columns)
        low_rank = (dot(x[d, 0], flat_d[:half]) + dot(x[d, 1], flat_d[half:])).astype(jnp.bfloat16)
        none = jnp.zeros_like(low_rank)
        key = (project(d, wk) + dot(jnp.where(low, low_rank, none), flat_u)).astype(jnp.bfloat16)
        value = (project(d, wv) + dot(jnp.where(low, none, low_rank), flat_u)).astype(jnp.bfloat16)
        return key, value

    def attend(d):
        key, value = keys_values(d)
        if d > 0:
            behind = jnp.maximum(me - d, 0)
            allowed = (me >= d) & (lookback[me] >= d) & (seg_ids[behind] == seg_ids[me])
            bias = jnp.where(allowed, 0.0, NEG_LARGE).astype(jnp.float32)
        for j in range(pairs):
            cols = slice(j * 128, (j + 1) * 128)
            outs, factors, totals = [], [], []
            for e in range(2):
                head = 2 * j + e
                s = dot_t(q_two[e, :, cols], key[:, cols])
                if d > 0:
                    s = s + bias
                m = jnp.broadcast_to(jnp.max(s, axis=1, keepdims=True), (rows, 128))
                if d > 0:
                    before = top[head]
                    m = jnp.maximum(before, m)
                    factor = jnp.exp(before - m)
                    factors.append(factor)
                parts = [jnp.exp(s[:, i:i + 128] - m) for i in range(0, rows, 128)]
                total = sum(parts[1:], parts[0])
                if d > 0:
                    total = total + tot[head] * factor
                if d == LOOK:
                    totals.append(jnp.sum(total, axis=1, keepdims=True))
                else:
                    top[head] = m
                    tot[head] = total
                w = jnp.concatenate([p.astype(jnp.bfloat16) for p in parts], axis=1)
                outs.append(dot(w, value[:, cols]))
            new = jnp.where(low, outs[0], outs[1])
            if d > 0:
                new = new + acc[:, cols] * jnp.where(low, factors[0], factors[1])
            if d == LOOK:
                new = new / jnp.where(low, totals[0], totals[1])
                out[:, cols] = new.astype(out.dtype)
            else:
                acc[:, cols] = new

    attend(0)
    hand_over(1)
    arrived(2)
    attend(2)
    arrived(1)
    attend(1)
    hand_over(3)
    arrived(3)
    attend(3)

    twin_copy(0).wait_send()
    for c in range(CHUNKS):
        for d in range(1, LOOK + 1):
            @pl.when(me >= d)
            def _():
                twin_copy(d, c).wait_send()

        @pl.when(me + 2 < n)
        def _():
            frame_copy(0, c, 2, 0, 2).wait_send()

        @pl.when(even)
        def _():
            frame_copy(1, c, 1, 0, 1).wait_send()

        @pl.when(me >= 2)
        def _():
            frame_copy(2, c, 3, 2, 1).wait_send()

        @pl.when(even & (me >= 2) & (me + 2 < n))
        def _():
            frame_copy(3, c, 3, 1, 2).wait_send()
    for k in range(1, n):
        for c in adapter_copies(k):
            c.wait_send()
    d_hand.wait_send()


def from_behind(block, axis, distance):
    devices = range(lax.axis_size(axis))
    route = [(i - distance, i) for i in devices if i - distance in devices]
    return lax.ppermute(block, axis, route)


def block_rules(seg_ids, lookback, position, distance, blocks_dev, block_len):
    query_first = position * blocks_dev
    key_first = (position - distance) * blocks_dev
    counter = jnp.arange(blocks_dev, dtype=jnp.int32)
    query_blocks = query_first + counter
    key_blocks = key_first + counter
    query_seg = lax.dynamic_slice_in_dim(seg_ids, query_first, blocks_dev)
    query_reach = lax.dynamic_slice_in_dim(lookback, query_first, blocks_dev)
    key_seg = lax.dynamic_slice_in_dim(seg_ids, jnp.maximum(key_first, 0), blocks_dev)
    allowed = key_blocks[None, :] >= query_blocks[:, None] - query_reach[:, None]
    allowed = allowed & (key_blocks[None, :] <= query_blocks[:, None])
    allowed = allowed & (key_seg[None, :] == query_seg[:, None]) & (key_blocks[None, :] >= 0)
    frames_dev = blocks_dev * block_len
    expanded = jnp.broadcast_to(
        allowed[:, None, :, None], (blocks_dev, block_len, blocks_dev, block_len)
    )
    return (jnp.any(allowed), expanded.reshape(frames_dev, frames_dev))


def attend(carried, query_heads, pair, allowed):
    run_max, run_sum, run_acc = carried
    frames_dev = query_heads.shape[0]
    heads_dev = query_heads.shape[1]
    key_heads = pair[0].reshape(frames_dev, heads_dev, HD)
    value_heads = pair[1].reshape(frames_dev, heads_dev, HD)
    scores = jnp.einsum(
        "qhe,khe->hqk", query_heads, key_heads, preferred_element_type=jnp.float32
    ) * HD ** (-0.5)
    masked = jnp.where(allowed[None], scores, NEG_LARGE)
    new_max = jnp.maximum(run_max, jnp.max(masked, axis=2))
    factor = jnp.exp(run_max - new_max)
    weights = jnp.where(allowed[None], jnp.exp(masked - new_max[:, :, None]), 0.0)
    new_sum = run_sum * factor + jnp.sum(weights, axis=2)
    update = jnp.einsum(
        "hqk,khe->hqe",
        weights.astype(jnp.bfloat16),
        value_heads,
        preferred_element_type=jnp.float32,
    )
    return (new_max, new_sum, run_acc * factor[:, :, None] + update)


def plain_body(
    frames, w_query, w_key, w_value, down_bank, up_bank, bank_row, lang_ids, seg_ids, lookback
):
    seq_count = lax.axis_size("seq")
    position = lax.axis_index("seq")
    frames_dev = frames.shape[0]
    blocks_dev = lang_ids.shape[0] // seq_count
    block_len = frames_dev // blocks_dev
    model_width = w_query.shape[0]
    columns = w_query.shape[1]
    heads_dev = columns // HD
    rank_two = down_bank.shape[2]
    rank_half = rank_two // 2
    wanted = jnp.transpose(jnp.take(bank_row, lang_ids, axis=0).reshape(seq_count, blocks_dev))
    picked = (wanted[:, :, None] == jnp.arange(down_bank.shape[0])).astype(jnp.bfloat16)
    down_send = jnp.einsum("wbl,lrc->wbrc", picked, down_bank)
    up_send = jnp.einsum("wbl,lrc->wbrc", picked, up_bank)
    down_got, up_got = (
        lax.all_to_all(down_send, "seq", split_axis=1, concat_axis=2, tiled=True),
        lax.all_to_all(up_send, "seq", split_axis=1, concat_axis=2, tiled=True),
    )
    down_mine = down_got.reshape(blocks_dev, model_width, rank_two)
    up_mine = up_got.reshape(blocks_dev, rank_two, columns)
    gathered = lax.all_gather(frames, "head", axis=1, tiled=True)
    queries = jnp.dot(gathered, w_query, preferred_element_type=jnp.float32).astype(jnp.bfloat16)
    block_rows = gathered.reshape(blocks_dev, block_len, model_width)
    lowrank = jnp.einsum(
        "bfd,bdr->bfr", block_rows, down_mine, preferred_element_type=jnp.float32
    ).astype(jnp.bfloat16)
    key_extra = jnp.einsum(
        "bfr,brc->bfc",
        lowrank[:, :, :rank_half],
        up_mine[:, :rank_half],
        preferred_element_type=jnp.float32,
    )
    value_extra = jnp.einsum(
        "bfr,brc->bfc",
        lowrank[:, :, rank_half:],
        up_mine[:, rank_half:],
        preferred_element_type=jnp.float32,
    )
    own_keys = (
        jnp.dot(gathered, w_key, preferred_element_type=jnp.float32)
        + key_extra.reshape(frames_dev, columns)
    ).astype(jnp.bfloat16)
    own_values = (
        jnp.dot(gathered, w_value, preferred_element_type=jnp.float32)
        + value_extra.reshape(frames_dev, columns)
    ).astype(jnp.bfloat16)
    own_pair = jnp.stack([own_keys, own_values])
    query_heads = queries.reshape(frames_dev, heads_dev, HD)
    initial = (
        jnp.full((heads_dev, frames_dev), NEG_LARGE, jnp.float32),
        jnp.zeros((heads_dev, frames_dev), jnp.float32),
        jnp.zeros((heads_dev, frames_dev, HD), jnp.float32),
    )

    def visit_tile(carried, pair, distance):
        nonempty, allowed = block_rules(
            seg_ids, lookback, position, distance, blocks_dev, block_len
        )
        return attend(carried, query_heads, pair, allowed)

    carried = visit_tile(initial, own_pair, 0)
    moving = own_pair
    for distance in range(1, 4):
        moving = from_behind(moving, "seq", 1)
        carried = visit_tile(carried, moving, distance)
    run_max, run_sum, run_acc = carried
    context = (run_acc / run_sum[:, :, None]).astype(jnp.bfloat16)
    return jnp.transpose(context, (1, 0, 2)).reshape(frames_dev, columns)


def body(frames, w_query, w_key, w_value, down_bank, up_bank, bank_row, lang_ids, seg_ids, lookback):
    n = lax.axis_size("seq")
    rows, half = frames.shape
    columns = w_query.shape[1]
    bank_rows, d_rows, rank_two = down_bank.shape
    u_rows = up_bank.shape[1]
    if n % 2 or d_rows % 32 or u_rows % 16 or lang_ids.shape[0] != n:
        return plain_body(
            frames, w_query, w_key, w_value, down_bank, up_bank, bank_row, lang_ids, seg_ids, lookback)
    bf16, f32 = jnp.bfloat16, jnp.float32
    d_shape, u_shape = (n, 2, d_rows // 2, rank_two), (n, u_rows, columns)
    banks = [down_bank.shape, up_bank.shape, (n - 1, d_rows // 2, rank_two), (n - 1, u_rows, columns)]
    hbm = pl.BlockSpec(memory_space=pltpu.HBM)
    dma = pltpu.SemaphoreType.DMA
    return pl.pallas_call(
        functools.partial(kernel, n),
        out_shape=jax.ShapeDtypeStruct((rows, columns), bf16),
        in_specs=[hbm] * 10,
        out_specs=pl.BlockSpec(memory_space=pltpu.VMEM),
        scratch_shapes=[
            *[pltpu.SMEM(t.shape, jnp.int32) for t in (bank_row, lang_ids, seg_ids, lookback)],
            pltpu.VMEM((LOOK + 1, 2, rows, half), bf16),
            *[pltpu.VMEM(w_query.shape, bf16)] * 3,
            pltpu.VMEM(d_shape, bf16),
            pltpu.VMEM(u_shape, bf16),
            *[pltpu.VMEM(s, bf16) for s in banks],
            pltpu.VMEM((2, rows, columns), bf16),
            pltpu.VMEM((rows, columns), f32),
            *[pltpu.VMEM((columns // HD, rows, 128), f32)] * 2,
            dma((10,)), dma((4, CHUNKS)), dma((LOOK, CHUNKS)), *[dma((LOOK + 1, CHUNKS))] * 2,
            dma((2, n - 1)), dma((2, n - 1)), dma, dma,
        ],
        compiler_params=pltpu.CompilerParams(
            collective_id=0, has_side_effects=True, vmem_limit_bytes=60 * 2 ** 20),
        cost_estimate=pl.CostEstimate(flops=6 * 10 ** 9, bytes_accessed=8 * 2 ** 20, transcendentals=2 ** 21),
    )(bank_row, lang_ids, seg_ids, lookback, frames, w_query, w_key, w_value, down_bank, up_bank)


def solution(mesh):
    in_specs = (
        P(("parts", "seq"), "head"),
        P(None, "head"),
        P(None, "head"),
        P(None, "head"),
        P(None, "seq", None),
        P(None, "seq", "head"),
        P(),
        P("parts"),
        P("parts"),
        P("parts"),
    )
    out_specs = P(("parts", "seq"), "head")
    return jax.shard_map(body, mesh=mesh, in_specs=in_specs, out_specs=out_specs, check_vma=False)
```

```python
import functools

import jax
import jax.numpy as jnp
from jax import lax
from jax.experimental import pallas as pl
from jax.experimental.pallas import tpu as pltpu
from jax.sharding import PartitionSpec as P

HD = 64
LOOK = 3
CHUNKS = 4
NEG_LARGE = -1e30
MESH = pl.DeviceIdType.MESH


def dot(a, b):
    return jnp.dot(a, b, preferred_element_type=jnp.float32)


def dot_t(a, b):
    return lax.dot_general(a, b, (((1,), (1,)), ((), ())), preferred_element_type=jnp.float32)


def kernel(
    n,
    bank_row_any, lang_any, seg_any, look_any, frames, w_query, w_key, w_value, down, up,
    out,
    bank_row, lang_ids, seg_ids, lookback,
    x, wq, wk, wv, d_mine, u_mine, d_bank, u_bank, d_send, u_send, q_two, acc, top, tot,
    local_sem, f_send, f_recv, t_send, t_recv, a_send, a_recv, dt_send, dt_recv,
):
    me = lax.axis_index("seq")
    h = lax.axis_index("head")
    rows, half = frames.shape
    columns = w_query.shape[1]
    pairs = columns // 128

    def local(src, dst, i):
        return pltpu.make_async_copy(src, dst, local_sem.at[i])

    own = local(frames, x.at[0, h], 0)
    tables = [
        local(bank_row_any, bank_row, 6), local(lang_any, lang_ids, 7),
        local(seg_any, seg_ids, 8), local(look_any, lookback, 9)]
    for c in tables:
        c.start()
    own.start()
    bank_d = local(down, d_bank, 4)
    bank_u = local(up, u_bank, 5)
    bank_d.start()
    bank_u.start()
    weights = [local(w_query, wq, 1), local(w_key, wk, 2), local(w_value, wv, 3)]
    for c in weights:
        c.start()

    barrier = pltpu.get_barrier_semaphore()
    twin = {"head": 1 - h}
    steps = range(1, n)
    pl.semaphore_signal(barrier, inc=1, device_id=twin, device_id_type=MESH)
    for k in steps:
        pl.semaphore_signal(barrier, inc=1, device_id={"seq": lax.rem(me + k, n)}, device_id_type=MESH)
    pl.semaphore_wait(barrier, len(steps) + 1)

    even = lax.rem(me, 2) == 0
    size = rows // CHUNKS

    def frame_copy(kind, c, slot, source, to):
        part = pl.ds(c * size, size)
        return pltpu.make_async_remote_copy(
            src_ref=frames.at[part] if source == 0 else x.at[source, h, part],
            dst_ref=x.at[slot, h, part], send_sem=f_send.at[kind, c], recv_sem=f_recv.at[slot - 1, c],
            device_id={"seq": lax.rem(me + to + n, n)}, device_id_type=MESH)

    def twin_copy(d, c=0):
        part = pl.ds(c * size, size) if d else pl.ds(0, rows)
        return pltpu.make_async_remote_copy(
            src_ref=x.at[d, h, part] if d else frames, dst_ref=x.at[d, h, part],
            send_sem=t_send.at[d, c], recv_sem=t_recv.at[d, c], device_id=twin, device_id_type=MESH)

    for c in range(CHUNKS):
        @pl.when(me + 2 < n)
        def _():
            frame_copy(0, c, 2, 0, 2).start()

        @pl.when(even)
        def _():
            frame_copy(1, c, 1, 0, 1).start()

    twin_copy(0).start()
    for c in tables:
        c.wait()

    def adapter_copies(k):
        to = {"seq": lax.rem(me + k, n)}
        return (
            pltpu.make_async_remote_copy(
                src_ref=d_send.at[k - 1], dst_ref=d_mine.at[me, h], send_sem=a_send.at[0, k - 1],
                recv_sem=a_recv.at[0, k - 1], device_id=to, device_id_type=MESH),
            pltpu.make_async_remote_copy(
                src_ref=u_send.at[k - 1], dst_ref=u_mine.at[me], send_sem=a_send.at[1, k - 1],
                recv_sem=a_recv.at[1, k - 1], device_id=to, device_id_type=MESH))

    def adapter_arrivals(k):
        source = lax.rem(me + n - k, n)
        return (
            pltpu.make_async_remote_copy(
                src_ref=d_send.at[k - 1], dst_ref=d_mine.at[source, h], send_sem=a_send.at[0, k - 1],
                recv_sem=a_recv.at[0, k - 1], device_id=twin, device_id_type=MESH),
            pltpu.make_async_remote_copy(
                src_ref=u_send.at[k - 1], dst_ref=u_mine.at[source], send_sem=a_send.at[1, k - 1],
                recv_sem=a_recv.at[1, k - 1], device_id=twin, device_id_type=MESH))

    piece = d_send.shape[1]
    first = pl.multiple_of(h * piece, piece)
    bank_d.wait()
    bank_u.wait()
    for k in range(1, n):
        row = bank_row[lang_ids[lax.rem(me + k, n)]]
        d_send[k - 1] = d_bank[row, pl.ds(first, piece), :]
        u_send[k - 1] = u_bank[row]
        for c in adapter_copies(k):
            c.start()
    row = bank_row[lang_ids[me]]
    d_mine[me, h] = d_bank[row, pl.ds(first, piece), :]
    u_mine[me] = u_bank[row]

    lane = lax.broadcasted_iota(jnp.int32, (rows, 128), 1)
    low = lane < HD

    own.wait()
    twin_copy(0).wait_recv()
    for c in weights:
        c.wait()

    def project(d, w):
        return dot(x[d, 0], w[:half]) + dot(x[d, 1], w[half:])

    q = (project(0, wq).astype(jnp.bfloat16).astype(jnp.float32) * HD ** (-0.5)).astype(jnp.bfloat16)
    for j in range(pairs):
        part = q[:, j * 128:(j + 1) * 128]
        q_two[0, :, j * 128:(j + 1) * 128] = jnp.where(low, part, jnp.zeros_like(part))
        q_two[1, :, j * 128:(j + 1) * 128] = jnp.where(low, jnp.zeros_like(part), part)

    own_base = (project(0, wk), project(0, wv))

    def hand_over(d):
        for c in range(CHUNKS):
            @pl.when(me >= d)
            def _():
                frame_copy(0, c, d, 0, 2).wait_recv()

            if d == 2:
                @pl.when(even & (me >= 2))
                def _():
                    frame_copy(2, c, 3, 2, 1).start()

                @pl.when((~even) & (me >= 3))
                def _():
                    frame_copy(2, c, 1, 2, -1).start()
            if d == 1:
                @pl.when(even & (me >= 2) & (me + 2 < n))
                def _():
                    frame_copy(3, c, 3, 1, 2).start()

            @pl.when(me >= d)
            def _():
                twin_copy(d, c).start()

        @pl.when(me < d)
        def _():
            x[d] = jnp.zeros(x.shape[1:], x.dtype)

    def arrived(d):
        for c in range(CHUNKS):
            @pl.when(me >= d)
            def _():
                twin_copy(d, c).wait_recv()

    hand_over(2)
    for k in range(1, n):
        for c in adapter_arrivals(k):
            c.wait_recv()
    d_hand = pltpu.make_async_remote_copy(
        src_ref=d_mine.at[:, h], dst_ref=d_mine.at[:, h], send_sem=dt_send, recv_sem=dt_recv,
        device_id=twin, device_id_type=MESH)
    d_hand.start()
    d_hand.wait_recv()

    def keys_values(d):
        flat_d = d_mine[...].reshape(2 * half, 128)
        flat_u = u_mine[...].reshape(128, columns)
        low_rank = (dot(x[d, 0], flat_d[:half]) + dot(x[d, 1], flat_d[half:])).astype(jnp.bfloat16)
        none = jnp.zeros_like(low_rank)
        base = (project(d, wk), project(d, wv)) if d else own_base
        key = (base[0] + dot(jnp.where(low, low_rank, none), flat_u)).astype(jnp.bfloat16)
        value = (base[1] + dot(jnp.where(low, none, low_rank), flat_u)).astype(jnp.bfloat16)
        return key, value

    def attend(d):
        key, value = keys_values(d)
        if d > 0:
            behind = jnp.maximum(me - d, 0)
            allowed = (me >= d) & (lookback[me] >= d) & (seg_ids[behind] == seg_ids[me])
            bias = jnp.where(allowed, 0.0, NEG_LARGE).astype(jnp.float32)
        for j in range(pairs):
            cols = slice(j * 128, (j + 1) * 128)
            outs, factors, totals = [], [], []
            for e in range(2):
                head = 2 * j + e
                s = dot_t(q_two[e, :, cols], key[:, cols])
                if d > 0:
                    s = s + bias
                m = jnp.broadcast_to(jnp.max(s, axis=1, keepdims=True), (rows, 128))
                if d > 0:
                    before = top[head]
                    m = jnp.maximum(before, m)
                    factor = jnp.exp(before - m)
                    factors.append(factor)
                parts = [jnp.exp(s[:, i:i + 128] - m) for i in range(0, rows, 128)]
                total = sum(parts[1:], parts[0])
                if d > 0:
                    total = total + tot[head] * factor
                if d == LOOK:
                    totals.append(jnp.sum(total, axis=1, keepdims=True))
                else:
                    top[head] = m
                    tot[head] = total
                w = jnp.concatenate([p.astype(jnp.bfloat16) for p in parts], axis=1)
                outs.append(dot(w, value[:, cols]))
            new = jnp.where(low, outs[0], outs[1])
            if d > 0:
                new = new + acc[:, cols] * jnp.where(low, factors[0], factors[1])
            if d == LOOK:
                new = new / jnp.where(low, totals[0], totals[1])
                out[:, cols] = new.astype(out.dtype)
            else:
                acc[:, cols] = new

    attend(0)
    hand_over(1)
    arrived(2)
    attend(2)
    arrived(1)
    attend(1)
    hand_over(3)
    arrived(3)
    attend(3)

    twin_copy(0).wait_send()
    for c in range(CHUNKS):
        for d in range(1, LOOK + 1):
            @pl.when(me >= d)
            def _():
                twin_copy(d, c).wait_send()

        @pl.when(me + 2 < n)
        def _():
            frame_copy(0, c, 2, 0, 2).wait_send()

        @pl.when(even)
        def _():
            frame_copy(1, c, 1, 0, 1).wait_send()

        @pl.when(me >= 2)
        def _():
            frame_copy(2, c, 3, 2, 1).wait_send()

        @pl.when(even & (me >= 2) & (me + 2 < n))
        def _():
            frame_copy(3, c, 3, 1, 2).wait_send()
    for k in range(1, n):
        for c in adapter_copies(k):
            c.wait_send()
    d_hand.wait_send()


def from_behind(block, axis, distance):
    devices = range(lax.axis_size(axis))
    route = [(i - distance, i) for i in devices if i - distance in devices]
    return lax.ppermute(block, axis, route)


def block_rules(seg_ids, lookback, position, distance, blocks_dev, block_len):
    query_first = position * blocks_dev
    key_first = (position - distance) * blocks_dev
    counter = jnp.arange(blocks_dev, dtype=jnp.int32)
    query_blocks = query_first + counter
    key_blocks = key_first + counter
    query_seg = lax.dynamic_slice_in_dim(seg_ids, query_first, blocks_dev)
    query_reach = lax.dynamic_slice_in_dim(lookback, query_first, blocks_dev)
    key_seg = lax.dynamic_slice_in_dim(seg_ids, jnp.maximum(key_first, 0), blocks_dev)
    allowed = key_blocks[None, :] >= query_blocks[:, None] - query_reach[:, None]
    allowed = allowed & (key_blocks[None, :] <= query_blocks[:, None])
    allowed = allowed & (key_seg[None, :] == query_seg[:, None]) & (key_blocks[None, :] >= 0)
    frames_dev = blocks_dev * block_len
    expanded = jnp.broadcast_to(
        allowed[:, None, :, None], (blocks_dev, block_len, blocks_dev, block_len)
    )
    return (jnp.any(allowed), expanded.reshape(frames_dev, frames_dev))


def attend(carried, query_heads, pair, allowed):
    run_max, run_sum, run_acc = carried
    frames_dev = query_heads.shape[0]
    heads_dev = query_heads.shape[1]
    key_heads = pair[0].reshape(frames_dev, heads_dev, HD)
    value_heads = pair[1].reshape(frames_dev, heads_dev, HD)
    scores = jnp.einsum(
        "qhe,khe->hqk", query_heads, key_heads, preferred_element_type=jnp.float32
    ) * HD ** (-0.5)
    masked = jnp.where(allowed[None], scores, NEG_LARGE)
    new_max = jnp.maximum(run_max, jnp.max(masked, axis=2))
    factor = jnp.exp(run_max - new_max)
    weights = jnp.where(allowed[None], jnp.exp(masked - new_max[:, :, None]), 0.0)
    new_sum = run_sum * factor + jnp.sum(weights, axis=2)
    update = jnp.einsum(
        "hqk,khe->hqe",
        weights.astype(jnp.bfloat16),
        value_heads,
        preferred_element_type=jnp.float32,
    )
    return (new_max, new_sum, run_acc * factor[:, :, None] + update)


def plain_body(
    frames, w_query, w_key, w_value, down_bank, up_bank, bank_row, lang_ids, seg_ids, lookback
):
    seq_count = lax.axis_size("seq")
    position = lax.axis_index("seq")
    frames_dev = frames.shape[0]
    blocks_dev = lang_ids.shape[0] // seq_count
    block_len = frames_dev // blocks_dev
    model_width = w_query.shape[0]
    columns = w_query.shape[1]
    heads_dev = columns // HD
    rank_two = down_bank.shape[2]
    rank_half = rank_two // 2
    wanted = jnp.transpose(jnp.take(bank_row, lang_ids, axis=0).reshape(seq_count, blocks_dev))
    picked = (wanted[:, :, None] == jnp.arange(down_bank.shape[0])).astype(jnp.bfloat16)
    down_send = jnp.einsum("wbl,lrc->wbrc", picked, down_bank)
    up_send = jnp.einsum("wbl,lrc->wbrc", picked, up_bank)
    down_got, up_got = (
        lax.all_to_all(down_send, "seq", split_axis=1, concat_axis=2, tiled=True),
        lax.all_to_all(up_send, "seq", split_axis=1, concat_axis=2, tiled=True),
    )
    down_mine = down_got.reshape(blocks_dev, model_width, rank_two)
    up_mine = up_got.reshape(blocks_dev, rank_two, columns)
    gathered = lax.all_gather(frames, "head", axis=1, tiled=True)
    queries = jnp.dot(gathered, w_query, preferred_element_type=jnp.float32).astype(jnp.bfloat16)
    block_rows = gathered.reshape(blocks_dev, block_len, model_width)
    lowrank = jnp.einsum(
        "bfd,bdr->bfr", block_rows, down_mine, preferred_element_type=jnp.float32
    ).astype(jnp.bfloat16)
    key_extra = jnp.einsum(
        "bfr,brc->bfc",
        lowrank[:, :, :rank_half],
        up_mine[:, :rank_half],
        preferred_element_type=jnp.float32,
    )
    value_extra = jnp.einsum(
        "bfr,brc->bfc",
        lowrank[:, :, rank_half:],
        up_mine[:, rank_half:],
        preferred_element_type=jnp.float32,
    )
    own_keys = (
        jnp.dot(gathered, w_key, preferred_element_type=jnp.float32)
        + key_extra.reshape(frames_dev, columns)
    ).astype(jnp.bfloat16)
    own_values = (
        jnp.dot(gathered, w_value, preferred_element_type=jnp.float32)
        + value_extra.reshape(frames_dev, columns)
    ).astype(jnp.bfloat16)
    own_pair = jnp.stack([own_keys, own_values])
    query_heads = queries.reshape(frames_dev, heads_dev, HD)
    initial = (
        jnp.full((heads_dev, frames_dev), NEG_LARGE, jnp.float32),
        jnp.zeros((heads_dev, frames_dev), jnp.float32),
        jnp.zeros((heads_dev, frames_dev, HD), jnp.float32),
    )

    def visit_tile(carried, pair, distance):
        nonempty, allowed = block_rules(
            seg_ids, lookback, position, distance, blocks_dev, block_len
        )
        return attend(carried, query_heads, pair, allowed)

    carried = visit_tile(initial, own_pair, 0)
    moving = own_pair
    for distance in range(1, 4):
        moving = from_behind(moving, "seq", 1)
        carried = visit_tile(carried, moving, distance)
    run_max, run_sum, run_acc = carried
    context = (run_acc / run_sum[:, :, None]).astype(jnp.bfloat16)
    return jnp.transpose(context, (1, 0, 2)).reshape(frames_dev, columns)


def body(frames, w_query, w_key, w_value, down_bank, up_bank, bank_row, lang_ids, seg_ids, lookback):
    n = lax.axis_size("seq")
    rows, half = frames.shape
    columns = w_query.shape[1]
    bank_rows, d_rows, rank_two = down_bank.shape
    u_rows = up_bank.shape[1]
    if n % 2 or d_rows % 32 or u_rows % 16 or lang_ids.shape[0] != n:
        return plain_body(
            frames, w_query, w_key, w_value, down_bank, up_bank, bank_row, lang_ids, seg_ids, lookback)
    bf16, f32 = jnp.bfloat16, jnp.float32
    d_shape, u_shape = (n, 2, d_rows // 2, rank_two), (n, u_rows, columns)
    banks = [down_bank.shape, up_bank.shape, (n - 1, d_rows // 2, rank_two), (n - 1, u_rows, columns)]
    hbm = pl.BlockSpec(memory_space=pltpu.HBM)
    dma = pltpu.SemaphoreType.DMA
    return pl.pallas_call(
        functools.partial(kernel, n),
        out_shape=jax.ShapeDtypeStruct((rows, columns), bf16),
        in_specs=[hbm] * 10,
        out_specs=pl.BlockSpec(memory_space=pltpu.VMEM),
        scratch_shapes=[
            *[pltpu.SMEM(t.shape, jnp.int32) for t in (bank_row, lang_ids, seg_ids, lookback)],
            pltpu.VMEM((LOOK + 1, 2, rows, half), bf16),
            *[pltpu.VMEM(w_query.shape, bf16)] * 3,
            pltpu.VMEM(d_shape, bf16),
            pltpu.VMEM(u_shape, bf16),
            *[pltpu.VMEM(s, bf16) for s in banks],
            pltpu.VMEM((2, rows, columns), bf16),
            pltpu.VMEM((rows, columns), f32),
            *[pltpu.VMEM((columns // HD, rows, 128), f32)] * 2,
            dma((10,)), dma((4, CHUNKS)), dma((LOOK, CHUNKS)), *[dma((LOOK + 1, CHUNKS))] * 2,
            dma((2, n - 1)), dma((2, n - 1)), dma, dma,
        ],
        compiler_params=pltpu.CompilerParams(
            collective_id=0, has_side_effects=True, vmem_limit_bytes=60 * 2 ** 20),
        cost_estimate=pl.CostEstimate(flops=6 * 10 ** 9, bytes_accessed=8 * 2 ** 20, transcendentals=2 ** 21),
    )(bank_row, lang_ids, seg_ids, lookback, frames, w_query, w_key, w_value, down_bank, up_bank)


def solution(mesh):
    in_specs = (
        P(("parts", "seq"), "head"),
        P(None, "head"),
        P(None, "head"),
        P(None, "head"),
        P(None, "seq", None),
        P(None, "seq", "head"),
        P(),
        P("parts"),
        P("parts"),
        P("parts"),
    )
    out_specs = P(("parts", "seq"), "head")
    return jax.shard_map(body, mesh=mesh, in_specs=in_specs, out_specs=out_specs, check_vma=False)
```
